256 devices in a mesh: img: 16 (over z_hi, y, core), txt: 16 (over z_lo, x).
Axes of the slice: x: 4, y: 4, z: 8 (z_hi: 2, z_lo: 4; z = z_hi * 4 + z_lo), core: 2. Of those that a mesh axis runs over, the one named last changes fastest.
Arguments:
- image: bfloat16 [16384, 1152], P(('img', 'txt')), may hold values from -0.23535156 to 0.23535156
- text: bfloat16 [16, 1024, 1152], P('txt', 'img'), may hold values from -0.23535156 to 0.23535156
- pair: int32 [16384], P(('img', 'txt')), may hold values from 0 to 16383, each once
- scale: float32 [1], replicated, may hold values from 5 to 15
- bias: float32 [1], replicated, may hold values from -4 to -1
Outputs:
- grad_image: float32 [16384, 1152], P(('img', 'txt'))
- grad_text: float32 [16, 1024, 1152], P('txt', 'img')
The draws below stay inside these ranges and needn't reach their ends.
Inputs may be any that keep to these rules, and one draw needn't show every extreme that they name: pair is a permutation of the text rows 0 to 16383.
All inputs are finite; a program needn't handle non-finite values.
Results may differ from the reference program's by a relative error of at most 0.0018.
Values may be sent and summed in bfloat16 or wider, within the bound.
A program may use at most 64 MiB of HBM per device.

```python
import jax
import jax.numpy as jnp
from jax import lax

D = 1152
IMAGES = 16384
IMG_BLK = 1024
TXT_BLK = 1024
N_IMG = 16
N_TXT = 16


def shard_levels(rng, shape, pieces, least, largest):
    level, own = 1.0, jax.random.fold_in(rng, 6)
    for axis_at, parts in pieces:
        draws = jnp.exp(jax.random.uniform(jax.random.fold_in(own, axis_at), (parts,), jnp.float32, least / len(pieces), largest / len(pieces)))
        level = level * jnp.repeat(draws, shape[axis_at] // parts).reshape([-1 if axis == axis_at else 1 for axis in range(len(shape))])
    return level


def scatter_about(key, shape, spread, reach, shards=(), kind=jnp.bfloat16):
    factor_of = shard_levels(key, shape, shards, -0.22, 0.18) if shards else 1.0
    values = jax.random.normal(key, shape, jnp.float32) * spread * factor_of
    return jnp.minimum(jnp.maximum(values, -reach), reach).astype(kind)


def setup_inputs(seed: int = 0) -> dict:
    splits = jax.random.split(jax.random.key(seed), 6)
    image = scatter_about(splits[0], (IMAGES, D), (1.7 * D ** -0.5), 0.23535156, ((0, 256),))
    text = scatter_about(splits[1], (N_TXT, TXT_BLK, D), (1.7 * D ** -0.5), 0.23535156, ((0, 16), (1, 16)))
    pair = jax.random.permutation(splits[2], IMAGES).astype(jnp.int32)
    scale = jnp.clip(jax.random.uniform(splits[3], (1,), jnp.float32, 5.0, 15.0), 5.0, 15.0)
    bias = jnp.clip(jax.random.uniform(splits[4], (1,), jnp.float32, -4.0, -1.0), -4.0, -1.0)
    return {"image": image, "text": text, "pair": pair, "scale": scale, "bias": bias}


def reference(image, text, pair, scale, bias):
    scale_v = scale[0]
    bias_v = bias[0]
    texts = text.reshape(IMAGES, D)
    columns = jnp.arange(IMAGES, dtype=jnp.int32)
    image_blocks = image.reshape(N_IMG, IMG_BLK, D)
    pair_blocks = pair.reshape(N_IMG, IMG_BLK)

    def one_block(acc, inputs):
        rows, partners = inputs
        logits = scale_v * jnp.dot(rows, texts.T, preferred_element_type=jnp.float32) + bias_v
        sign = jnp.where(partners[:, None] == columns[None, :], jnp.float32(1.0), jnp.float32(-1.0))
        coeff = (scale_v * (-sign) * jax.nn.sigmoid(-sign * logits)).astype(jnp.bfloat16)
        image_grad = jnp.dot(coeff, texts, preferred_element_type=jnp.float32)
        text_tile = jnp.dot(coeff.T, rows, preferred_element_type=jnp.float32)
        return acc + text_tile, image_grad

    start = jnp.zeros((IMAGES, D), jnp.float32)
    text_sum, image_grads = lax.scan(one_block, start, (image_blocks, pair_blocks))
    return image_grads.reshape(IMAGES, D), text_sum.reshape(N_TXT, TXT_BLK, D)
```

```python
import jax
import jax.numpy as jnp
from jax import lax
from jax.experimental import pallas as pl
from jax.experimental.pallas import tpu as pltpu
from jax.sharding import PartitionSpec as P

ROWS = 64
HALF = 32
QUART = 16
BLK = 256
N_SEM = 160
TOP = 32766.0
POS = {4: 0, 3: 1, 5: 2, 2: 3, 6: 4, 1: 5, 7: 6, 0: 7}
SEND_ROWS = 1408


def xrow(half, major, minor):
    return major * 256 + half * 128 + minor * HALF


def yrow(dz, dc):
    return POS[dz] * 128 + dc * ROWS


def kernel(
    image, text, pair, scale, bias, out_i, out_t,
    xs, ys, partner, column, coef, coef_t, gi, gt, sib, sbuf, rbuf, sscale, rscale,
    local_sem, send_sem, recv_sem,
):
    img = lax.axis_index("img")
    txt = lax.axis_index("txt")
    core = lax.rem(img, 2)
    y = lax.rem(lax.div(img, 2), 4)
    x = lax.rem(txt, 4)
    z = lax.div(img, 8) * 4 + lax.div(txt, 4)
    width = xs.shape[1]

    def device(x, y, z, core):
        return {"img": lax.div(z, 4) * 8 + y * 2 + core, "txt": lax.rem(z, 4) * 4 + x}

    step = {1: 1, -1: 3}
    near = {}
    for way in (1, -1):
        near["x", way] = device(lax.rem(x + step[way], 4), y, z, core)
        near["y", way] = device(x, lax.rem(y + step[way], 4), z, core)
        near["z", way] = device(x, y, lax.rem(z + (1 if way == 1 else 7), 8), core)
    sibling = device(x, y, z, 1 - core)

    count = [0]
    sent = []

    def message(src, dst, to):
        at = count[0]
        count[0] += 1
        return pltpu.make_async_remote_copy(
            src_ref=src, dst_ref=dst, send_sem=send_sem.at[at], recv_sem=recv_sem.at[at],
            device_id=to, device_id_type=pl.DeviceIdType.MESH,
        )

    def start(m):
        m.start()
        sent.append(m)

    locals_ = [
        pltpu.make_async_copy(image.at[pl.ds(0, HALF)], xs.at[pl.ds(xrow(0, 0, 0), HALF)], local_sem.at[0]),
        pltpu.make_async_copy(image.at[pl.ds(HALF, HALF)], xs.at[pl.ds(xrow(1, 0, 0), HALF)], local_sem.at[1]),
        pltpu.make_async_copy(text.at[0], ys.at[pl.ds(yrow(0, 0), ROWS)], local_sem.at[2]),
    ]
    for c in locals_:
        c.start()
    barrier = pltpu.get_barrier_semaphore()
    for to in [*near.values(), sibling]:
        pl.semaphore_signal(barrier, inc=1, device_id=to, device_id_type=pl.DeviceIdType.MESH)

    own = pair[...]
    own_a, own_b = own[:, :HALF], own[:, HALF:]
    partner[pl.ds(0, 4)] = jnp.broadcast_to(jnp.concatenate([own_a] * 4, axis=1), (4, 128))
    partner[pl.ds(4, 4)] = jnp.broadcast_to(jnp.concatenate([own_b] * 4, axis=1), (4, 128))
    for dz in range(8):
        zz = lax.rem(z + dz, 8)
        for dc in range(2):
            cc = core if dc == 0 else 1 - core
            d = device(x, y, zz, cc)
            base = d["txt"] * 1024 + d["img"] * ROWS
            column[pl.ds(yrow(dz, dc), ROWS)] = base + lax.broadcasted_iota(jnp.int32, (ROWS, 128), 0)
    pl.semaphore_wait(barrier, 7)
    for c in locals_:
        c.wait()

    axes = {0: ("x", "y"), 1: ("y", "x")}

    def xpart(half, major, minor, off=0, rows=HALF):
        return xs.at[pl.ds(xrow(half, major, minor) + off, rows)]

    def ypart(dz, dc, off=0, rows=ROWS):
        return ys.at[pl.ds(yrow(dz, dc) + off, rows)]

    def ppart(dy, dx, n=1):
        return partner.at[pl.ds((dy * 4 + dx) * 8, 8 * n)]

    g1, g2, g3, g4 = {}, {}, {}, {}
    for h in (0, 1):
        a1, a2 = axes[h]
        g1[h, 1] = message(xpart(h, 0, 0), xpart(h, 0, 3), near[a1, 1])
        g1[h, -1] = message(xpart(h, 0, 0), xpart(h, 0, 1), near[a1, -1])
        g2[h, 1] = message(xpart(h, 0, 3, 0, QUART), xpart(h, 0, 2, 0, QUART), near[a1, 1])
        g2[h, -1] = message(xpart(h, 0, 1, QUART, QUART), xpart(h, 0, 2, QUART, QUART), near[a1, -1])
        for mi in range(4):
            g3[h, 1, mi] = message(xpart(h, 0, mi), xpart(h, 3, mi), near[a2, 1])
            g3[h, -1, mi] = message(xpart(h, 0, mi), xpart(h, 1, mi), near[a2, -1])
        for mi in (0, 1):
            g4[h, mi] = message(xpart(h, 3, mi), xpart(h, 2, mi), near[a2, 1])
        for mi in (3, 2):
            g4[h, mi] = message(xpart(h, 1, mi), xpart(h, 2, mi), near[a2, -1])
    p1p = message(ppart(0, 0), ppart(0, 3), near["x", 1])
    p1m = message(ppart(0, 0), ppart(0, 1), near["x", -1])
    p2 = message(ppart(0, 3), ppart(0, 2), near["x", 1])
    p3p = message(ppart(0, 0, 4), ppart(3, 0, 4), near["y", 1])
    p3m = message(ppart(0, 0, 4), ppart(1, 0, 4), near["y", -1])
    p4 = message(ppart(3, 0, 4), ppart(2, 0, 4), near["y", 1])
    zg = {}
    for k in range(3):
        zg[1, k] = message(ypart((8 - k) % 8, 0), ypart(7 - k, 0), near["z", 1])
        zg[-1, k] = message(ypart(k, 0), ypart(k + 1, 0), near["z", -1])
    zg[1, 3] = message(ypart(5, 0, 0, HALF), ypart(4, 0, 0, HALF), near["z", 1])
    zg[-1, 3] = message(ypart(3, 0, HALF, HALF), ypart(4, 0, HALF, HALF), near["z", -1])
    sg = {dz: message(ypart(dz, 0), ypart(dz, 1), sibling) for dz in range(8)}

    scale_v = scale[0]
    bias_v = bias[0]
    lane = lax.broadcasted_iota(jnp.int32, (1, 128), 1)

    def partners(k):
        def pick(refs):
            r = refs[3]
            for i in (2, 1, 0):
                r = jnp.where(lane < 32 * (i + 1), refs[i], r)
            return r

        a = pick([partner[pl.ds((k * 4 + dx) * 8, 1)] for dx in range(4)])
        b = pick([partner[pl.ds((dy * 4 + k) * 8 + 4, 1)] for dy in range(4)])
        return jnp.concatenate([a, b], axis=1)

    def coefficients(k, first, last):
        who = partners(k)
        cols = pl.ds(k * BLK, BLK)

        @pl.loop(first, last)
        def _(c):
            rows = pl.ds(pl.multiple_of(c * BLK, BLK), BLK)
            logits = lax.dot_general(
                ys[rows], xs[cols], (((1,), (1,)), ((), ())), preferred_element_type=jnp.float32
            )
            logits = scale_v * logits + bias_v
            col = column[rows]
            match = jnp.concatenate([col, col], axis=1) == who
            value = scale_v * jax.nn.sigmoid(jnp.where(match, -logits, logits))
            value = jnp.where(match, -value, value).astype(jnp.bfloat16)
            coef_t[rows, cols] = value
            coef[cols, rows] = value.T

    for h in (0, 1):
        start(g1[h, 1])
        start(g1[h, -1])
    start(zg[1, 0])
    start(zg[-1, 0])
    start(p1p)
    start(p1m)
    for h in (0, 1):
        start(g3[h, 1, 0])
        start(g3[h, -1, 0])
    start(sg[0])
    for h in (0, 1):
        g1[h, 1].wait_recv()
        start(g2[h, 1])
        start(g3[h, 1, 3])
        start(g3[h, -1, 3])
        g1[h, -1].wait_recv()
        start(g2[h, -1])
        start(g3[h, 1, 1])
        start(g3[h, -1, 1])
    p1p.wait_recv()
    start(p2)
    p1m.wait_recv()
    for way in (1, -1):
        zg[way, 0].wait_recv()
        start(zg[way, 1])
    start(sg[7])
    start(sg[1])
    p2.wait_recv()
    start(p3p)
    start(p3m)
    for h in (0, 1):
        g2[h, 1].wait_recv()
        g2[h, -1].wait_recv()
        start(g3[h, 1, 2])
        start(g3[h, -1, 2])
    for h in (0, 1):
        g3[h, 1, 0].wait_recv()
        start(g4[h, 0])
        g3[h, -1, 3].wait_recv()
        start(g4[h, 3])
    p3p.wait_recv()
    start(p4)
    p3m.wait_recv()
    p4.wait_recv()
    sg[0].wait_recv()
    sg[7].wait_recv()
    coefficients(0, 3, 4)
    for way in (1, -1):
        zg[way, 1].wait_recv()
        start(zg[way, 2])
    start(sg[6])
    start(sg[2])
    for h in (0, 1):
        g3[h, 1, 1].wait_recv()
        start(g4[h, 1])
        g3[h, -1, 2].wait_recv()
        start(g4[h, 2])
    sg[1].wait_recv()
    sg[6].wait_recv()
    coefficients(0, 2, 3)
    for way in (1, -1):
        zg[way, 2].wait_recv()
        start(zg[way, 3])
    start(sg[5])
    start(sg[3])
    for h in (0, 1):
        g3[h, -1, 0].wait_recv()
        g3[h, -1, 1].wait_recv()
    coefficients(1, 2, 4)
    for h in (0, 1):
        g3[h, 1, 3].wait_recv()
        g3[h, 1, 2].wait_recv()
    coefficients(3, 2, 4)
    for way in (1, -1):
        zg[way, 3].wait_recv()
    start(sg[4])
    for dz in (2, 5, 3):
        sg[dz].wait_recv()
    for k in (0, 1, 3):
        coefficients(k, 1, 2)
    sg[4].wait_recv()
    for k in (0, 1, 3):
        coefficients(k, 0, 1)
    for h in (0, 1):
        for mi in range(4):
            g4[h, mi].wait_recv()
    coefficients(2, 0, 4)

    def image_rows(k):
        rows = pl.ds(k * BLK, BLK)
        gi[rows] = jnp.dot(coef[rows], ys[...], preferred_element_type=jnp.float32)

    def text_rows(c):
        rows = pl.ds(c * BLK, BLK)
        gt[rows] = jnp.dot(coef_t[rows], xs[...], preferred_element_type=jnp.float32)

    sm = {}

    def sibling_send(dz):
        sm[dz] = message(gt.at[pl.ds(yrow(dz, 1), ROWS)], sib.at[pl.ds(POS[dz] * ROWS, ROWS)], sibling)
        start(sm[dz])

    place = [0]
    slots = [0]

    def spread(s):
        s = jnp.concatenate([s, s], axis=0)
        return jnp.concatenate([s] * (width // 128), axis=1)

    def incoming(adds):
        return [(spread(rscale[pl.ds(a.slot * 8, 8)]), a.row + off) for a, off in adds]

    def total(acc, at, got, extra, i):
        v = acc[pl.ds(at + i * QUART, QUART)]
        for s, row in got:
            v = v + rbuf[pl.ds(row + i * QUART, QUART)].astype(jnp.float32) * s
        if extra is not None:
            v = v + sib[pl.ds(extra + i * QUART, QUART)]
        return v

    class Packed:
        def __init__(self, acc, at, rows, to, adds=(), extra=None):
            self.row, self.slot = place[0], slots[0]
            place[0] += rows
            slots[0] += 1
            got = incoming(adds)
            top = jnp.zeros((8, 128), jnp.float32)
            for i in range(rows // QUART):
                v = total(acc, at, got, extra, i)
                if got or extra is not None:
                    acc[pl.ds(at + i * QUART, QUART)] = v
                v = jnp.abs(v)
                for r in range(2):
                    for j in range(width // 128):
                        top = jnp.maximum(top, v[r * 8 : r * 8 + 8, j * 128 : j * 128 + 128])
            top = jnp.maximum(top, 1e-30)
            sscale[pl.ds(self.slot * 8, 8)] = top * (1.0 / TOP)
            inverse = spread(TOP / top)
            for i in range(rows // QUART):
                q = jnp.round(acc[pl.ds(at + i * QUART, QUART)] * inverse)
                sbuf[pl.ds(self.row + i * QUART, QUART)] = q.astype(jnp.int32).astype(jnp.int16)
            there = pl.ds(self.row, rows)
            note = pl.ds(self.slot * 8, 8)
            self.data = message(sbuf.at[there], rbuf.at[there], to)
            self.note = message(sscale.at[note], rscale.at[note], to)
            start(self.data)
            start(self.note)

        def wait(self):
            self.data.wait_recv()
            self.note.wait_recv()

    m, n = {}, {}

    def plane(h, name, major, pair_of, way, adds=()):
        m[h, name] = Packed(gi, xrow(h, major, 2 * pair_of), 2 * HALF, near[axes[h][1], way], adds)

    def line(h, name, minor, quarter, way, adds=()):
        n[h, name] = Packed(
            gi, xrow(h, 0, minor) + quarter * QUART, QUART, near[axes[h][0], way], [*base_adds(h, minor, quarter), *adds]
        )

    def base_adds(h, minor, quarter):
        off = (minor % 2) * HALF + quarter * QUART
        return [(m[h, name], off) for name in ((4, 5) if minor < 2 else (2, 6))]

    zs = {}

    def ring(way, half, dz, adds=()):
        zs[way, half, dz] = Packed(
            gt, yrow(dz, 0) + half * HALF, HALF, near["z", way], adds, POS[dz] * ROWS + half * HALF
        )

    def ring_next(way, half, dz):
        before = zs[way, half, dz + way]
        before.wait()
        ring(way, half, dz, [(before, 0)])

    text_rows(0)
    sibling_send(4)
    sibling_send(3)
    image_rows(2)
    for h in (0, 1):
        plane(h, 1, 2, 0, 1)
        plane(h, 3, 2, 1, -1)
    text_rows(1)
    sibling_send(5)
    sibling_send(2)
    sm[4].wait_recv()
    ring(1, 0, 4)
    ring(-1, 1, 4)
    image_rows(1)
    for h in (0, 1):
        plane(h, 2, 1, 1, 1)
    image_rows(3)
    for h in (0, 1):
        plane(h, 4, 3, 0, -1)
    sm[3].wait_recv()
    ring(1, 1, 3)
    sm[5].wait_recv()
    ring(-1, 0, 5)
    text_rows(2)
    sibling_send(6)
    sibling_send(1)
    for h in (0, 1):
        m[h, 1].wait()
        plane(h, 5, 1, 0, 1, [(m[h, 1], 0)])
        m[h, 3].wait()
        plane(h, 6, 3, 1, -1, [(m[h, 3], 0)])
    ring_next(1, 0, 3)
    ring_next(-1, 1, 5)
    sm[2].wait_recv()
    ring_next(1, 1, 2)
    sm[6].wait_recv()
    ring_next(-1, 0, 6)
    text_rows(3)
    sibling_send(7)
    sibling_send(0)
    image_rows(0)
    ring_next(1, 0, 2)
    ring_next(-1, 1, 6)
    sm[1].wait_recv()
    ring_next(1, 1, 1)
    sm[7].wait_recv()
    ring_next(-1, 0, 7)
    for h in (0, 1):
        m[h, 2].wait()
        m[h, 6].wait()
        line(h, 1, 2, 0, 1)
        line(h, 3, 2, 1, -1)
    for h in (0, 1):
        m[h, 4].wait()
        m[h, 5].wait()
        line(h, 4, 3, 0, -1)
        line(h, 2, 1, 1, 1)
    ring_next(1, 0, 1)
    ring_next(-1, 1, 7)
    for h in (0, 1):
        n[h, 1].wait()
        line(h, 5, 1, 0, 1, [(n[h, 1], 0)])
        n[h, 3].wait()
        line(h, 6, 3, 1, -1, [(n[h, 3], 0)])
    sm[0].wait_recv()
    for half in (0, 1):
        ends = [zs[1, half, 1], zs[-1, half, 7]]
        for e in ends:
            e.wait()
        got = incoming([(e, 0) for e in ends])
        for i in range(2):
            v = total(gt, yrow(0, 0) + half * HALF, got, POS[0] * ROWS + half * HALF, i)
            out_t[0, pl.ds(half * HALF + i * QUART, QUART)] = v
    for h in (0, 1):
        for quarter, names in ((0, (4, 5)), (1, (2, 6))):
            for name in names:
                n[h, name].wait()
            got = incoming([*base_adds(h, 0, quarter), *[(n[h, name], 0) for name in names]])
            v = total(gi, xrow(h, 0, 0) + quarter * QUART, got, None, 0)
            out_i[pl.ds(h * HALF + quarter * QUART, QUART)] = v
    for c in sent:
        c.wait_send()


def local(image, text, pair, scale, bias):
    width = image.shape[1]
    f32, bf16, i32, i16 = jnp.float32, jnp.bfloat16, jnp.int32, jnp.int16
    hbm = pl.BlockSpec(memory_space=pl.ANY)
    vmem = pl.BlockSpec(memory_space=pltpu.VMEM)
    smem = pl.BlockSpec(memory_space=pltpu.SMEM)
    return pl.pallas_call(
        kernel,
        out_shape=(
            jax.ShapeDtypeStruct(image.shape, f32),
            jax.ShapeDtypeStruct(text.shape, f32),
        ),
        in_specs=[hbm, hbm, vmem, smem, smem],
        out_specs=(vmem, vmem),
        scratch_shapes=[
            pltpu.VMEM((1024, width), bf16),
            pltpu.VMEM((1024, width), bf16),
            pltpu.VMEM((128, 128), i32),
            pltpu.VMEM((1024, 128), i32),
            pltpu.VMEM((1024, 1024), bf16),
            pltpu.VMEM((1024, 1024), bf16),
            pltpu.VMEM((1024, width), f32),
            pltpu.VMEM((1024, width), f32),
            pltpu.VMEM((512, width), f32),
            pltpu.VMEM((SEND_ROWS, width), i16),
            pltpu.VMEM((SEND_ROWS, width), i16),
            pltpu.VMEM((40 * 8, 128), f32),
            pltpu.VMEM((40 * 8, 128), f32),
            pltpu.SemaphoreType.DMA((3,)),
            pltpu.SemaphoreType.DMA((N_SEM,)),
            pltpu.SemaphoreType.DMA((N_SEM,)),
        ],
        compiler_params=pltpu.CompilerParams(
            collective_id=0, has_side_effects=True, vmem_limit_bytes=52 * 1024 * 1024
        ),
    )(image, text, pair.reshape(1, -1), scale, bias)


def solution(mesh):
    return jax.shard_map(
        local,
        mesh=mesh,
        in_specs=(P(("img", "txt"), None), P("txt", "img", None), P(("img", "txt")), P(), P()),
        out_specs=(P(("img", "txt"), None), P("txt", "img", None)),
        check_vma=False,
    )
```

```python
import jax
import jax.numpy as jnp
from jax import lax
from jax.experimental import pallas as pl
from jax.experimental.pallas import tpu as pltpu
from jax.sharding import PartitionSpec as P

ROWS = 64
HALF = 32
QUART = 16
BLK = 256
N_SEM = 160
TOP = 32000.0
POS = {4: 0, 3: 1, 5: 2, 2: 3, 6: 4, 1: 5, 7: 6, 0: 7}


def xrow(half, major, minor):
    return major * 256 + half * 128 + minor * HALF


def yrow(dz, dc):
    return POS[dz] * 128 + dc * ROWS


def kernel(
    image, text, pair, scale, bias, out_i, out_t,
    xs, ys, own, known, partner, column, coef, coef_t, gi, gt, sib, sbuf, rbuf,
    local_sem, send_sem, recv_sem,
):
    img = lax.axis_index("img")
    txt = lax.axis_index("txt")
    core = lax.rem(img, 2)
    y = lax.rem(lax.div(img, 2), 4)
    x = lax.rem(txt, 4)
    z = lax.div(img, 8) * 4 + lax.div(txt, 4)
    width = xs.shape[1]
    tiles = width // 128

    def device(x, y, z, core):
        return {"img": lax.div(z, 4) * 8 + y * 2 + core, "txt": lax.rem(z, 4) * 4 + x}

    near = {}
    for way, by in ((1, 1), (-1, 3), (2, 2)):
        near["x", way] = device(lax.rem(x + by, 4), y, z, core)
        near["y", way] = device(x, lax.rem(y + by, 4), z, core)
    for way, by in ((1, 1), (-1, 7)):
        near["z", way] = device(x, y, lax.rem(z + by, 8), core)
    sibling = device(x, y, z, 1 - core)

    count = [0]
    sent = []

    def message(src, dst, to):
        at = count[0]
        count[0] += 1
        return pltpu.make_async_remote_copy(
            src_ref=src, dst_ref=dst, send_sem=send_sem.at[at], recv_sem=recv_sem.at[at],
            device_id=to, device_id_type=pl.DeviceIdType.MESH,
        )

    def start(m):
        m.start()
        sent.append(m)

    barrier = pltpu.get_barrier_semaphore()
    for to in [*near.values(), sibling]:
        pl.semaphore_signal(barrier, inc=1, device_id=to, device_id_type=pl.DeviceIdType.MESH)
    locals_ = [
        pltpu.make_async_copy(image.at[pl.ds(0, HALF)], xs.at[pl.ds(xrow(0, 0, 0), HALF)], local_sem.at[0]),
        pltpu.make_async_copy(image.at[pl.ds(HALF, HALF)], xs.at[pl.ds(xrow(1, 0, 0), HALF)], local_sem.at[1]),
        pltpu.make_async_copy(text.at[0], ys.at[pl.ds(yrow(0, 0), ROWS)], local_sem.at[2]),
        pltpu.make_async_copy(pair, own, local_sem.at[3]),
    ]
    for c in locals_:
        c.start()
    for dz in range(8):
        zz = lax.rem(z + dz, 8)
        for dc in range(2):
            d = device(x, y, zz, core if dc == 0 else 1 - core)
            base = d["txt"] * 1024 + d["img"] * ROWS
            column[pl.ds(yrow(dz, dc), ROWS)] = base + lax.broadcasted_iota(jnp.int32, (ROWS, 128), 0)
    locals_[3].wait()
    mine = own[...]
    for at, part in ((0, mine[:, :HALF]), (1, mine[:, HALF:])):
        known[pl.ds(at, 1)] = jnp.concatenate([part] * 4, axis=1)
    for c in locals_[:3]:
        c.wait()
    pl.semaphore_wait(barrier, 9)

    axes = {0: ("x", "y"), 1: ("y", "x")}
    both = (0, 1)

    def xpart(half, major, minor, off=0, rows=HALF):
        return xs.at[pl.ds(xrow(half, major, minor) + off, rows)]

    def ypart(dz, dc, off=0, rows=ROWS):
        return ys.at[pl.ds(yrow(dz, dc) + off, rows)]

    def kpart(dx):
        return known.at[pl.ds(dx * 8, 8)]

    def ppart(dy):
        return partner.at[pl.ds(dy * 8, 8)]

    first, fwd, second, last = {}, {}, {}, {}
    for h in both:
        a1, a2 = axes[h]
        for s in range(2):
            o = s * QUART
            first[h, 1, s] = message(xpart(h, 0, 0, o, QUART), xpart(h, 0, 3, o, QUART), near[a1, 1])
            first[h, -1, s] = message(xpart(h, 0, 0, o, QUART), xpart(h, 0, 1, o, QUART), near[a1, -1])
        fwd[h, 1] = message(xpart(h, 0, 3, 0, QUART), xpart(h, 0, 2, 0, QUART), near[a1, 1])
        fwd[h, -1] = message(xpart(h, 0, 1, QUART, QUART), xpart(h, 0, 2, QUART, QUART), near[a1, -1])
        for mi in range(4):
            second[h, 1, mi] = message(xpart(h, 0, mi), xpart(h, 3, mi), near[a2, 1])
            second[h, -1, mi] = message(xpart(h, 0, mi), xpart(h, 1, mi), near[a2, -1])
        last[h, 1, 0] = message(xpart(h, 3, 0), xpart(h, 2, 0), near[a2, 1])
        last[h, -1, 3] = message(xpart(h, 1, 3), xpart(h, 2, 3), near[a2, -1])
        for mi in (1, 2):
            last[h, 1, mi] = message(xpart(h, 3, mi, 0, QUART), xpart(h, 2, mi, 0, QUART), near[a2, 1])
            last[h, -1, mi] = message(xpart(h, 1, mi, QUART, QUART), xpart(h, 2, mi, QUART, QUART), near[a2, -1])
    pfirst = {w: message(kpart(0), kpart((-w) % 4), near["x", w]) for w in (1, -1, 2)}
    psecond = {w: message(ppart(0), ppart((-w) % 4), near["y", w]) for w in (1, -1, 2)}
    zg = {}
    for k in range(4):
        for s in range(4):
            o = s * QUART
            if k < 3 or s < 2:
                zg[1, k, s] = message(ypart((8 - k) % 8, 0, o, QUART), ypart(7 - k, 0, o, QUART), near["z", 1])
            if k < 3 or s > 1:
                zg[-1, k, s] = message(ypart(k, 0, o, QUART), ypart(k + 1, 0, o, QUART), near["z", -1])
    sg = {dz: message(ypart(dz, 0), ypart(dz, 1), sibling) for dz in range(8)}

    scale_v = scale[0]
    bias_v = bias[0]
    lane = lax.broadcasted_iota(jnp.int32, (1, 128), 1)

    def partners(k):
        def pick(refs):
            r = refs[3]
            for i in (2, 1, 0):
                r = jnp.where(lane < 32 * (i + 1), refs[i], r)
            return r

        a = pick([partner[pl.ds(k * 8 + dx * 2, 1)] for dx in range(4)])
        b = pick([partner[pl.ds(dy * 8 + k * 2 + 1, 1)] for dy in range(4)])
        return jnp.concatenate([a, b], axis=1)

    def coefficients(k, begin, end):
        who = partners(k)
        cols = pl.ds(k * BLK, BLK)
        for at in range(begin, end, BLK):
            rows = pl.ds(at, min(BLK, end - at))
            logits = lax.dot_general(
                ys[rows], xs[cols], (((1,), (1,)), ((), ())), preferred_element_type=jnp.float32
            )
            logits = scale_v * logits + bias_v
            col = column[rows]
            match = jnp.concatenate([col, col], axis=1) == who
            value = scale_v * jax.nn.sigmoid(jnp.where(match, -logits, logits))
            value = jnp.where(match, -value, value).astype(jnp.bfloat16)
            coef_t[rows, cols] = value
            coef[cols, rows] = value.T

    def ring_hop(k, order):
        for s in order:
            for way, sub in ((1, s), (-1, 3 - s)):
                zg[way, k - 1, sub].wait_recv()
                if (way, k, sub) in zg:
                    start(zg[way, k, sub])

    def own_first(s):
        for h in both:
            start(first[h, 1, s])
            start(first[h, -1, 1 - s])

    def own_ring(s):
        start(zg[1, 0, s])
        start(zg[-1, 0, 3 - s])

    own_first(0)
    for w in (2, 1, -1):
        start(pfirst[w])
    own_ring(0)
    own_first(1)
    own_ring(1)
    for h in both:
        start(second[h, 1, 0])
        start(second[h, -1, 0])
    own_ring(2)
    own_ring(3)
    start(sg[0])
    for h in both:
        first[h, 1, 0].wait_recv()
        start(fwd[h, 1])
        first[h, -1, 1].wait_recv()
        start(fwd[h, -1])
    ring_hop(1, [0])
    for w in (1, -1, 2):
        pfirst[w].wait_recv()
    for dx in range(4):
        partner[pl.ds(dx * 2, 2)] = known[pl.ds(dx * 8, 2)]
    for w in (2, 1, -1):
        start(psecond[w])
    for h in both:
        first[h, 1, 1].wait_recv()
        start(second[h, 1, 3])
        start(second[h, -1, 3])
        first[h, -1, 0].wait_recv()
        start(second[h, 1, 1])
        start(second[h, -1, 1])
    ring_hop(1, [1, 2])
    ring_hop(1, [3])
    start(sg[7])
    start(sg[1])
    for h in both:
        for w in (1, -1):
            fwd[h, w].wait_recv()
        for w in (1, -1):
            start(second[h, w, 2])
    for h in both:
        second[h, 1, 0].wait_recv()
        start(last[h, 1, 0])
    ring_hop(2, [0, 1])
    for dz in (0, 7, 1):
        sg[dz].wait_recv()
    for w in (1, -1, 2):
        psecond[w].wait_recv()
    coefficients(0, 640, 1024)
    ring_hop(2, [2, 3])
    start(sg[6])
    start(sg[2])
    for h in both:
        second[h, -1, 3].wait_recv()
        start(last[h, -1, 3])
    for h in both:
        for w in (1, -1):
            second[h, w, 1].wait_recv()
            start(last[h, w, 1])
    ring_hop(3, [0, 1])
    for h in both:
        for w in (1, -1):
            second[h, w, 2].wait_recv()
            start(last[h, w, 2])
    for h in both:
        second[h, 1, 3].wait_recv()
        second[h, -1, 0].wait_recv()
    for dz in (6, 2):
        sg[dz].wait_recv()
    coefficients(0, 384, 640)
    coefficients(1, 384, 1024)
    ring_hop(3, [2, 3])
    start(sg[5])
    start(sg[3])
    coefficients(3, 384, 1024)
    for s in (0, 1):
        zg[1, 3, s].wait_recv()
        zg[-1, 3, 3 - s].wait_recv()
    start(sg[4])
    for dz in (5, 3):
        sg[dz].wait_recv()
    for k in (0, 1, 3):
        coefficients(k, 128, 384)
    for m in last.values():
        m.wait_recv()
    coefficients(2, 128, 1024)
    sg[4].wait_recv()
    for k in range(4):
        coefficients(k, 0, 128)

    def image_rows(k):
        rows = pl.ds(k * BLK, BLK)
        gi[rows] = jnp.dot(coef[rows], ys[...], preferred_element_type=jnp.float32)

    def text_rows(c):
        rows = pl.ds(c * BLK, BLK)
        gt[rows] = jnp.dot(coef_t[rows], xs[...], preferred_element_type=jnp.float32)

    sm = {}

    def sibling_send(dz):
        sm[dz] = message(gt.at[pl.ds(yrow(dz, 1), ROWS)], sib.at[pl.ds(POS[dz] * ROWS, ROWS)], sibling)
        start(sm[dz])

    place = [0]

    def spread(s):
        s = jnp.concatenate([s, s], axis=0) if s.shape[0] == 8 else s
        return jnp.concatenate([s] * tiles, axis=1)

    def total(acc, at, rows, adds, extra=None):
        units = [spread(jnp.exp2(rbuf[a.place + a.rows // QUART * tiles].astype(jnp.float32))) for a, _ in adds]
        out = []
        for i in range(rows // QUART):
            v = acc[pl.ds(at + i * QUART, QUART)]
            for (a, off), unit in zip(adds, units):
                t = a.place + (off // QUART + i) * tiles
                q = jnp.concatenate([rbuf[t + j] for j in range(tiles)], axis=1)
                v = v + q.astype(jnp.float32) * unit
            if extra is not None:
                v = v + sib[pl.ds(extra + i * QUART, QUART)]
            out.append(v)
        return out

    class Packed:
        def __init__(self, acc, at, rows, to, adds=(), extra=None):
            self.place, self.rows = place[0], rows
            n = rows // QUART * tiles
            place[0] += n + 1
            vs = total(acc, at, rows, adds, extra)
            top = jnp.full((8, 128), 1e-30, jnp.float32)
            for v in vs:
                v = jnp.abs(v)
                for r in range(2):
                    for j in range(tiles):
                        top = jnp.maximum(top, v[r * 8 : r * 8 + 8, j * 128 : j * 128 + 128])
            unit = jnp.ceil(jnp.log2(top * (1.0 / TOP)))
            per = spread(jnp.exp2(-unit))
            for i, v in enumerate(vs):
                q = jnp.round(v * per).astype(jnp.int32).astype(jnp.int16)
                for j in range(tiles):
                    sbuf[self.place + i * tiles + j] = q[:, j * 128 : j * 128 + 128]
            sbuf[self.place + n] = jnp.concatenate([unit, unit], axis=0).astype(jnp.int32).astype(jnp.int16)
            there = pl.ds(self.place, n + 1)
            self.data = message(sbuf.at[there], rbuf.at[there], to)
            start(self.data)

        def wait(self):
            self.data.wait_recv()

    m, n, zs = {}, {}, {}

    def plane(h, way, k, mi):
        adds = []
        if (h, way, 2, mi) in m and k != 2:
            m[h, way, 2, mi].wait()
            adds = [(m[h, way, 2, mi], 0)]
        m[h, way, k, mi] = Packed(gi, xrow(h, k, mi), HALF, near[axes[h][1], way], adds)

    def planes(way, k, mi):
        for h in both:
            plane(h, way, k, mi)

    def came(h, mi):
        got = [m[h, 1, 1, mi], m[h, -1, 3, mi]]
        for g in got:
            g.wait()
        return [(g, 0) for g in got]

    def line(h, mi):
        n[h, mi] = Packed(gi, xrow(h, 0, mi), HALF, near[axes[h][0], {1: 1, 3: -1, 2: 2}[mi]], came(h, mi))

    def ring(k, order):
        for s in order:
            for way, sub in ((1, s), (-1, 3 - s)):
                dz = k if way == 1 else 8 - k
                before = zs.get((way, k + 1, sub))
                if before is not None:
                    before.wait()
                zs[way, k, sub] = Packed(
                    gt, yrow(dz, 0) + sub * QUART, QUART, near["z", way],
                    [] if before is None else [(before, 0)], POS[dz] * ROWS + sub * QUART,
                )

    text_rows(0)
    sibling_send(4)
    sibling_send(3)
    image_rows(2)
    planes(1, 2, 2)
    planes(-1, 2, 3)
    sm[4].wait_recv()
    ring(4, [0, 1])
    planes(1, 2, 1)
    planes(-1, 2, 0)
    text_rows(1)
    sibling_send(5)
    sibling_send(2)
    image_rows(1)
    planes(1, 1, 3)
    sm[3].wait_recv()
    sm[5].wait_recv()
    ring(3, [2, 3])
    image_rows(3)
    planes(-1, 3, 2)
    ring(3, [0, 1])
    planes(1, 1, 2)
    planes(-1, 3, 3)
    text_rows(2)
    sibling_send(6)
    sibling_send(1)
    planes(-1, 3, 1)
    planes(1, 1, 1)
    sm[2].wait_recv()
    sm[6].wait_recv()
    ring(2, [2, 3])
    planes(1, 1, 0)
    planes(-1, 3, 0)
    ring(2, [0, 1])
    text_rows(3)
    sibling_send(7)
    sibling_send(0)
    image_rows(0)
    for h in both:
        line(h, 2)
        line(h, 3)
    sm[1].wait_recv()
    sm[7].wait_recv()
    ring(1, [2, 3])
    for h in both:
        line(h, 1)
    ring(1, [0, 1])
    for h in both:
        adds = came(h, 0)
        for mi in (3, 2, 1):
            n[h, mi].wait()
            adds.append((n[h, mi], 0))
        for i, v in enumerate(total(gi, xrow(h, 0, 0), HALF, adds)):
            out_i[pl.ds(h * HALF + i * QUART, QUART)] = v
    sm[0].wait_recv()
    for sub in (2, 3, 0, 1):
        ends = [zs[1, 1, sub], zs[-1, 1, sub]]
        for e in ends:
            e.wait()
        v = total(gt, yrow(0, 0) + sub * QUART, QUART, [(e, 0) for e in ends], POS[0] * ROWS + sub * QUART)
        out_t[0, pl.ds(sub * QUART, QUART)] = v[0]
    for c in sent:
        c.wait_send()


def local(image, text, pair, scale, bias):
    width = image.shape[1]
    tiles = 88 * (width // 128) + 58
    f32, bf16, i32, i16 = jnp.float32, jnp.bfloat16, jnp.int32, jnp.int16
    hbm = pl.BlockSpec(memory_space=pltpu.HBM)
    vmem = pl.BlockSpec(memory_space=pltpu.VMEM)
    smem = pl.BlockSpec(memory_space=pltpu.SMEM)
    return pl.pallas_call(
        kernel,
        out_shape=(
            jax.ShapeDtypeStruct(image.shape, f32),
            jax.ShapeDtypeStruct(text.shape, f32),
        ),
        in_specs=[hbm, hbm, hbm, smem, smem],
        out_specs=(vmem, vmem),
        scratch_shapes=[
            pltpu.VMEM((1024, width), bf16),
            pltpu.VMEM((1024, width), bf16),
            pltpu.VMEM((1, ROWS), i32),
            pltpu.VMEM((32, 128), i32),
            pltpu.VMEM((32, 128), i32),
            pltpu.VMEM((1024, 128), i32),
            pltpu.VMEM((1024, 1024), bf16),
            pltpu.VMEM((1024, 1024), bf16),
            pltpu.VMEM((1024, width), f32),
            pltpu.VMEM((1024, width), f32),
            pltpu.VMEM((512, width), f32),
            pltpu.VMEM((tiles, QUART, 128), i16),
            pltpu.VMEM((tiles, QUART, 128), i16),
            pltpu.SemaphoreType.DMA((4,)),
            pltpu.SemaphoreType.DMA((N_SEM,)),
            pltpu.SemaphoreType.DMA((N_SEM,)),
        ],
        compiler_params=pltpu.CompilerParams(
            collective_id=0, has_side_effects=True, vmem_limit_bytes=52 * 1024 * 1024
        ),
    )(*[pltpu.with_memory_space_constraint(a, pltpu.HBM) for a in (image, text, pair.reshape(1, -1))], scale, bias)


def solution(mesh):
    return jax.shard_map(
        local,
        mesh=mesh,
        in_specs=(P(("img", "txt"), None), P("txt", "img", None), P(("img", "txt")), P(), P()),
        out_specs=(P(("img", "txt"), None), P("txt", "img", None)),
        check_vma=False,
    )
```
